32 devices in a mesh: bond: 8 (over y, x, core), mpo: 4 (over z).
Axes of the slice: x: 2, y: 2, z: 4, core: 2. Of those that a mesh axis runs over, the one named last changes fastest.
Arguments:
- carried: bfloat16 [198, 8192], P(None, 'bond'), may hold values from -6 to 6
- site_tensors: bfloat16 [2, 8192, 4, 8192], P(None, 'bond', 'mpo'), may hold values from -0.09375 to 0.09375
- operator_tensors: bfloat16 [2, 4, 66, 264], replicated, may hold values from -0.375 to 0.375
- rotation: bfloat16 [2, 8192, 4, 8192], P(None, 'bond', 'mpo'), may hold values from -0.09375 to 0.09375
- kept_columns: int32 [2, 8192], replicated, may hold values from 0 to 32767, as said below
Outputs:
- rotated_state: bfloat16 [198, 8192], P(None, 'bond')
- truncation_gram: float32 [2, 198, 198], replicated
The draws below stay inside these ranges and needn't reach their ends.
Inputs may be any that keep to these rules, and one draw needn't show every extreme that they name: `kept_columns`: each row holds 8192 distinct values; value r * 4 + t names right-bond index r and physical index t.
All inputs are finite; a program needn't handle non-finite values.
Results may differ from the reference program's by a relative error of at most 0.035.
Values may be sent and summed in bfloat16 or wider, within the bound.
A program may use at most 128 MiB of HBM per device.

```python
import jax
import jax.numpy as jnp
from jax import lax

BOND_DIM = 8192
PHYSICAL = 4
MPO_BOND = 66
LEFT_ROWS = 3
SITE_COUNT = 2
ROW_TOTAL = 198
N_BOND = 8


def draw_kept_columns(key, part):
    listed = []
    for position in range(SITE_COUNT):
        shuffled = jax.random.permutation(jax.random.fold_in(key, 11 + position), PHYSICAL * BOND_DIM)
        listed.append(shuffled[:BOND_DIM].astype(jnp.int32))
    return jnp.stack(listed)


def raised(drawn, stream_key, source, target, parts, factor):
    owner, partner = [(jnp.arange(drawn.shape[dim]) // (drawn.shape[dim] // parts)).reshape([-1 if axis == dim else 1 for axis in range(drawn.ndim)]) for dim in (source, target)]
    chosen = jax.random.permutation(stream_key, parts)[partner]
    strong = (owner == chosen) | (owner == (partner + parts // 2) % parts)
    return jnp.where(strong, factor * drawn, drawn)


def steps_of(own_key, extent, cuts, smallest, largest):
    def one(dim, parts):
        steps = jax.random.uniform(jax.random.fold_in(jax.random.fold_in(own_key, 6), dim), (parts,), jnp.float32, smallest / len(cuts), largest / len(cuts))
        return jnp.repeat(jnp.exp(steps), extent[dim] // parts).reshape((-1,) + (1,) * (len(extent) - dim - 1))

    gain = one(*cuts[0])
    for cut in cuts[1:]:
        gain = gain * one(*cut)
    return gain


def normal_values(stream_key, extent, scale, limit, cuts=(), held_as=jnp.bfloat16):
    gain = steps_of(stream_key, extent, cuts, -0.22, 0.18) if cuts else 1.0
    entries = jax.random.normal(stream_key, extent, jnp.float32) * scale * gain
    return jnp.minimum(jnp.maximum(entries, -limit), limit).astype(held_as)


def noise_with(rng, dims, scale, limit, pieces, heavy, held_as=jnp.bfloat16):
    array = scale * jax.random.normal(rng, dims, jnp.float32)
    if pieces:
        array = array * steps_of(rng, dims, pieces, -0.22, 0.18)
    return jnp.clip(raised(array, jax.random.fold_in(rng, 3), *heavy), -limit, limit).astype(held_as)


def setup_inputs(seed: int = 0) -> dict:
    key_of = jax.random.split(jax.random.key(seed), 6)
    carried = normal_values(key_of[0], (ROW_TOTAL, BOND_DIM), 1.0, 6.0, ((1, 8),))
    site_tensors = noise_with(key_of[1], (SITE_COUNT, BOND_DIM, PHYSICAL, BOND_DIM), BOND_DIM ** -0.5, 0.09375, ((1, 8), (2, 4)), (1, 3, 8, 2.0))
    operator_tensors = normal_values(key_of[2], (SITE_COUNT, PHYSICAL, MPO_BOND, PHYSICAL * MPO_BOND), (PHYSICAL * MPO_BOND) ** -0.5, 0.375)
    rotation = noise_with(key_of[3], (SITE_COUNT, BOND_DIM, PHYSICAL, BOND_DIM), BOND_DIM ** -0.5, 0.09375, ((1, 8), (2, 4)), (1, 3, 8, 2.0))
    kept_columns = draw_kept_columns(jax.random.fold_in(key_of[5], 71), 0)
    return {"carried": carried, "site_tensors": site_tensors, "operator_tensors": operator_tensors, "rotation": rotation, "kept_columns": kept_columns}


def reference(carried, site_tensors, operator_tensors, rotation, kept_columns):
    row_count = carried.shape[0]
    width = carried.shape[1]
    block_width = width // N_BOND
    state = carried
    gram_list = []
    for position in range(SITE_COUNT):
        tensor = site_tensors[position].reshape(width, PHYSICAL * width)

        def accumulate(running, number, state=state, tensor=tensor):
            offset = (number * block_width).astype(jnp.int32)
            left_block = lax.dynamic_slice_in_dim(state, offset, block_width, 1)
            right_block = lax.dynamic_slice_in_dim(tensor, offset, block_width, 0)
            rounded = jnp.dot(left_block, right_block, preferred_element_type=jnp.float32).astype(jnp.bfloat16)
            rounded = lax.optimization_barrier(rounded)
            return running + rounded.astype(jnp.float32), None

        summed, _ = lax.scan(accumulate, jnp.zeros((row_count, PHYSICAL * width), jnp.float32),
                             jnp.arange(N_BOND, dtype=jnp.int32))
        contracted = summed.astype(jnp.bfloat16).reshape(LEFT_ROWS, MPO_BOND, PHYSICAL, width)
        mixed_rows = jnp.einsum('lasr,sac->lcr', contracted.astype(jnp.float32),
                                operator_tensors[position].astype(jnp.float32),
                                precision=lax.Precision.HIGHEST)
        mixed_rows = mixed_rows.reshape(LEFT_ROWS, PHYSICAL, MPO_BOND, width)
        chosen = jnp.zeros((PHYSICAL * width,), jnp.float32).at[kept_columns[position]].set(1.0)
        chosen = chosen.reshape(width, PHYSICAL)
        kept_rows = (mixed_rows * chosen.T[None, :, None, :]).astype(jnp.bfloat16)
        kept_float = kept_rows.astype(jnp.float32)
        gram_matrix = jnp.einsum('ltar,mtbr->lamb', kept_float, kept_float,
                                 precision=lax.Precision.HIGHEST).reshape(row_count, row_count) / width
        gram_list.append(gram_matrix)
        flattened = kept_rows.transpose(0, 2, 3, 1).reshape(row_count, width * PHYSICAL)
        rotated = jnp.dot(flattened, rotation[position].reshape(width * PHYSICAL, width),
                          preferred_element_type=jnp.float32)
        state = rotated.astype(jnp.bfloat16)
    return state, jnp.stack(gram_list)
```

```python
import functools

import jax
import jax.numpy as jnp
from jax import lax
from jax.experimental import pallas as pl
from jax.experimental.pallas import tpu as pltpu
from jax.sharding import PartitionSpec as P

LEFT_ROWS = 3
SITE_COUNT = 2
MESH = pl.DeviceIdType.MESH
F32 = jnp.float32
BF16 = jnp.bfloat16


def flip(index, bit):
    return index + (1 - 2 * ((index // (1 << bit)) % 2)) * (1 << bit)


def xor_bits(index, other, bits):
    out = 0
    for b in range(bits):
        out = out + (((index // (1 << b)) % 2 + (other // (1 << b)) % 2) % 2) * (1 << b)
    return out


def reverse_bits(index, bits):
    out = 0
    for b in range(bits):
        out = out + ((index // (1 << b)) % 2) * (1 << (bits - 1 - b))
    return out


def z_roles():
    z = lax.axis_index("mpo")
    is_mid = (z == 1) | (z == 2)
    inner = jnp.where(z == 0, 1, 2)
    outer = jnp.where(z == 1, 0, 3)
    return z, is_mid, inner, outer, 3 - z


def site_kernel(bits, chunks, site, mixing, *refs):
    if mixing:
        (state, weight, ops, mask, out, gram,
         wbuf, psend, own, prec, xrec, cg, zsend, zrec,
         wsem, pss, prs, xss, xrs, zss, zrs) = refs
    else:
        (state, weight, out,
         wbuf, psend, own, prec, xrec, zown, zin, zsum, zrec,
         wsem, pss, prs, xss, xrs, zss, zrs) = refs
    chips = 1 << bits
    depth = state.shape[1]
    rows = state.shape[0]
    block = weight.shape[2] // (2 * chips)
    width = block // chunks
    half = width // 2
    j = lax.axis_index("bond")
    me, core = j // 2, j % 2
    z, is_mid, inner, outer, across = z_roles()
    is_end = jnp.logical_not(is_mid)

    def weight_copy(c, other, r):
        dest = 2 * xor_bits(me, r, bits) + (1 - core if other else core)
        start = pl.multiple_of(dest * block + c * width, 128)
        slot = (c * 2 + (0 if other else 1)) * chips + r
        return pltpu.make_async_copy(
            weight.at[site, :, pl.ds(start, width)], wbuf.at[slot], wsem.at[slot]
        )

    for c in range(chunks):
        for other in (True, False):
            @pl.loop(0, chips)
            def _(r):
                weight_copy(c, other, r).start()

    barrier = pltpu.get_barrier_semaphore()

    def greet(bond, mpo):
        pl.semaphore_signal(barrier, inc=1, device_id=(bond, mpo), device_id_type=MESH)

    greet(2 * me + 1 - core, z)
    for b in range(bits):
        greet(2 * flip(me, b) + core, z)

    @pl.when(is_mid)
    def _():
        greet(j, outer)
        greet(j, across)
        pl.semaphore_wait(barrier, bits + 3)

    @pl.when(is_end)
    def _():
        greet(j, inner)
        pl.semaphore_wait(barrier, bits + 2)

    def remote(src, dst, ss, rs, bond, mpo):
        return pltpu.make_async_remote_copy(
            src_ref=src, dst_ref=dst, send_sem=ss, recv_sem=rs,
            device_id=(bond, mpo), device_id_type=MESH,
        )

    def pair_copy(c):
        return remote(psend.at[c], prec.at[c], pss.at[c], prs.at[c], 2 * me + 1 - core, z)

    def xy_copy(c, step, side):
        n = chips >> (step + 1)
        bit = bits - 1 - step if side == 0 else step
        return remote(
            own.at[c, side, pl.ds(n, n)], xrec.at[c, side, pl.ds(n, n)],
            xss.at[c, step, side], xrs.at[c, step, side], 2 * flip(me, bit) + core, z,
        )

    def multiply(c):
        for other, target in ((True, psend), (False, own)):
            @pl.loop(0, chips)
            def _(r):
                weight_copy(c, other, r).wait()
                slot = (c * 2 + (0 if other else 1)) * chips + r
                product = jnp.dot(state[...], wbuf[slot], preferred_element_type=F32).astype(BF16)
                target[c, 0, r] = product[:, :half]
                target[c, 1, reverse_bits(r, bits)] = product[:, half:]

            if other:
                pair_copy(c).start()

    def pair_sum(c):
        pair_copy(c).wait_recv()
        for side in range(2):
            own[c, side] = (own[c, side].astype(F32) + prec[c, side].astype(F32)).astype(BF16)
            xy_copy(c, 0, side).start()

    def xy_sum(c, step):
        n = chips >> (step + 1)
        parts = []
        for side in range(2):
            xy_copy(c, step, side).wait_recv()
            total = (own[c, side, pl.ds(0, n)].astype(F32)
                     + xrec[c, side, pl.ds(n, n)].astype(F32)).astype(BF16)
            if step < bits - 1:
                own[c, side, pl.ds(0, n)] = total
                xy_copy(c, step + 1, side).start()
            else:
                parts.append(total[0])
        return parts

    columns = [pl.ds(c * width, width) for c in range(chunks)]

    if mixing:
        def z_end_copy(c, slot):
            return remote(cg.at[c, slot], cg.at[c, slot],
                          zss.at[c, 0], zrs.at[c, 0], j, jnp.where(is_mid, outer, inner))

        def z_own_copy(c, slot):
            return remote(cg.at[c, slot], cg.at[c, slot],
                          zss.at[c, 1], zrs.at[c, 1], j, jnp.where(is_mid, across, inner))

        def z_pass_copy(c, slot):
            return remote(cg.at[c, slot], cg.at[c, slot],
                          zss.at[c, 2], zrs.at[c, 2], j, jnp.where(is_mid, across, inner))

        def z_back_copy(c):
            return remote(zsend.at[c], zrec.at[c],
                          zss.at[c, 3], zrs.at[c, 3], j, jnp.where(is_mid, outer, inner))

        def z_first(c, parts):
            cg[c, z, :, pl.ds(0, half)] = parts[0]
            cg[c, z, :, pl.ds(half, half)] = parts[1]

            @pl.when(is_end)
            def _():
                z_end_copy(c, z).start()

            @pl.when(is_mid)
            def _():
                z_own_copy(c, z).start()

        def z_second(c):
            @pl.when(is_mid)
            def _():
                z_end_copy(c, outer).wait_recv()
                z_pass_copy(c, outer).start()

        def mix(c, which):
            total = jnp.dot(ops[site, which, 0], cg[c, 0], preferred_element_type=F32)
            for s in range(1, 4):
                total += jnp.dot(ops[site, which, s], cg[c, s], preferred_element_type=F32)
            return total

        def keep(c, mixed):
            kept = (mixed * mask[:, columns[c]]).astype(BF16)
            out[:, columns[c]] = kept
            square = lax.dot_general(kept, kept, (((1,), (1,)), ((), ())),
                                     preferred_element_type=F32)
            if c == 0:
                gram[...] = square
            else:
                gram[...] += square

        def z_third(c):
            @pl.when(is_mid)
            def _():
                z_own_copy(c, across).wait_recv()
                z_pass_copy(c, 3 - outer).wait_recv()
                zsend[c] = mix(c, 1).astype(BF16)
                z_back_copy(c).start()
                keep(c, mix(c, 0))

        def z_fourth(c):
            @pl.when(is_end)
            def _():
                z_back_copy(c).wait_recv()
                keep(c, zrec[c].astype(F32))

        end_sends = (lambda c: z_end_copy(c, z),)
        mid_sends = (lambda c: z_own_copy(c, z), lambda c: z_pass_copy(c, outer), z_back_copy)
    else:
        def z_end_copy(c):
            return remote(zown.at[c], zin.at[c],
                          zss.at[c, 0], zrs.at[c, 0], j, jnp.where(is_mid, outer, inner))

        def z_mid_copy(c):
            return remote(zsum.at[c], zrec.at[c],
                          zss.at[c, 1], zrs.at[c, 1], j, jnp.where(is_mid, across, inner))

        def z_back_copy(c):
            return remote(zown.at[c], zin.at[c],
                          zss.at[c, 2], zrs.at[c, 2], j, jnp.where(is_mid, outer, inner))

        def z_first(c, parts):
            zown[c, :, pl.ds(0, half)] = parts[0]
            zown[c, :, pl.ds(half, half)] = parts[1]

            @pl.when(is_end)
            def _():
                z_end_copy(c).start()

        def z_second(c):
            @pl.when(is_mid)
            def _():
                z_end_copy(c).wait_recv()
                zsum[c] = (zown[c].astype(F32) + zin[c].astype(F32)).astype(BF16)
                z_mid_copy(c).start()

        def z_third(c):
            @pl.when(is_mid)
            def _():
                z_mid_copy(c).wait_recv()
                total = (zsum[c].astype(F32) + zrec[c].astype(F32)).astype(BF16)
                zown[c] = total
                z_back_copy(c).start()
                out[:, columns[c]] = total

        def z_fourth(c):
            @pl.when(is_end)
            def _():
                z_back_copy(c).wait_recv()
                out[:, columns[c]] = zin[c]

        end_sends, mid_sends = (z_end_copy,), (z_mid_copy, z_back_copy)

    stages = [multiply, pair_sum]
    for step in range(bits - 1):
        stages.append(functools.partial(xy_sum, step=step))
    stages += [lambda c: z_first(c, xy_sum(c, bits - 1)), z_second, z_third, z_fourth]
    for t in range(chunks + len(stages) - 1):
        for number, stage in enumerate(stages):
            if 0 <= t - number < chunks:
                stage(t - number)

    for c in range(chunks):
        pair_copy(c).wait_send()
        for step in range(bits):
            for side in range(2):
                xy_copy(c, step, side).wait_send()

        @pl.when(is_end)
        def _():
            for copy in end_sends:
                copy(c).wait_send()

        @pl.when(is_mid)
        def _():
            for copy in mid_sends:
                copy(c).wait_send()


def apply_site(bits, site, mixing, state, weight, *extra):
    rows, depth = state.shape
    chips = 1 << bits
    block = weight.shape[2] // (2 * chips)
    chunks = max(1, block // 256)
    width = block // chunks
    half = width // 2
    vmem = pl.BlockSpec(memory_space=pltpu.VMEM)
    parts = pltpu.VMEM((chunks, 2, chips, rows, half), BF16)
    piece = pltpu.VMEM((chunks, rows, width), BF16)
    out_shape = [jax.ShapeDtypeStruct((rows, block), BF16)]
    if mixing:
        out_shape.append(jax.ShapeDtypeStruct((rows, rows), F32))
        z_scratch = [pltpu.VMEM((chunks, 4, rows, width), BF16), piece, piece]
    else:
        z_scratch = [piece] * 4
    dma = pltpu.SemaphoreType.DMA
    z_copies = 4 if mixing else 3
    return pl.pallas_call(
        functools.partial(site_kernel, bits, chunks, site, mixing),
        out_shape=out_shape,
        in_specs=[vmem, pl.BlockSpec(memory_space=pl.ANY)] + [vmem] * len(extra),
        out_specs=[vmem] * len(out_shape),
        scratch_shapes=[
            pltpu.VMEM((2 * chips * chunks, depth, width), BF16),
            parts, parts, parts, parts,
            *z_scratch,
            dma((2 * chips * chunks,)),
            dma((chunks,)), dma((chunks,)),
            dma((chunks, bits, 2)), dma((chunks, bits, 2)),
            dma((chunks, z_copies)), dma((chunks, z_copies)),
        ],
        compiler_params=pltpu.CompilerParams(
            collective_id=2 * site + (0 if mixing else 1),
            has_side_effects=True,
            vmem_limit_bytes=48 * 1024 * 1024,
        ),
        cost_estimate=pl.CostEstimate(
            flops=2 * rows * depth * weight.shape[2],
            bytes_accessed=2 * depth * weight.shape[2],
            transcendentals=0,
        ),
    )(state, weight, *extra)


def operator_blocks(operator_tensors, rows):
    bonds = operator_tensors.shape[2]
    z, is_mid, inner, outer, across = z_roles()
    found = []
    for t in (z, jnp.where(is_mid, outer, inner)):
        found.append(lax.dynamic_slice_in_dim(operator_tensors, t * bonds, bonds, 3))
    ops = jnp.stack(found, axis=1).swapaxes(3, 4)
    keep = ((0, 0),) * 3
    blocks = []
    for l in range(LEFT_ROWS):
        place = (l * bonds, rows - (l + 1) * bonds)
        blocks.append(jnp.pad(ops, keep + (place, place)))
    return functools.reduce(jnp.add, blocks)


def chosen_columns(kept_columns, physical, block):
    index = kept_columns // physical - lax.axis_index("bond") * block
    mine = (kept_columns % physical) == lax.axis_index("mpo")
    high = jnp.where(mine & (index >= 0), index // 128, -1)
    low = index % 128
    high = (high[:, :, None] == jnp.arange(block // 128)).astype(BF16)
    low = (low[:, :, None] == jnp.arange(128)).astype(BF16)
    marks = jnp.einsum("khi,khj->kij", high, low, preferred_element_type=F32)
    return marks.reshape(kept_columns.shape[0], 1, block)


def solution(mesh):
    bits = (mesh.shape["bond"] // 2).bit_length() - 1

    def on_device(carried, site_tensors, operator_tensors, rotation, kept_columns):
        row_count, block = carried.shape
        rows = -(-row_count // 16) * 16
        physical = operator_tensors.shape[1]
        sites = site_tensors.reshape(site_tensors.shape[0], block, -1)
        turns = rotation.reshape(rotation.shape[0], block, -1)
        ops = operator_blocks(operator_tensors, rows)
        mask = chosen_columns(kept_columns, physical, block)
        state = jnp.pad(carried, ((0, rows - row_count), (0, 0)))
        grams = []
        for site in range(SITE_COUNT):
            kept, gram = apply_site(bits, site, True, state, sites, ops, mask[site])
            gram = gram[:row_count, :row_count] / (block * mesh.shape["bond"])
            grams.append(lax.psum(gram, ("bond", "mpo")))
            (state,) = apply_site(bits, site, False, kept, turns)
        return state[:row_count], jnp.stack(grams)

    return jax.shard_map(
        on_device,
        mesh=mesh,
        in_specs=(
            P(None, "bond"),
            P(None, "bond", "mpo", None),
            P(),
            P(None, "bond", "mpo", None),
            P(),
        ),
        out_specs=(P(None, "bond"), P()),
        check_vma=False,
    )
```

```python
import functools

import jax
import jax.numpy as jnp
from jax import lax
from jax.experimental import pallas as pl
from jax.experimental.pallas import tpu as pltpu
from jax.sharding import PartitionSpec as P

LEFT_ROWS = 3
SITE_COUNT = 2
MESH = pl.DeviceIdType.MESH
F32 = jnp.float32
BF16 = jnp.bfloat16


def flip(index, bit):
    return index + (1 - 2 * ((index // (1 << bit)) % 2)) * (1 << bit)


def xor_bits(index, other, bits):
    out = 0
    for b in range(bits):
        out = out + (((index // (1 << b)) % 2 + (other // (1 << b)) % 2) % 2) * (1 << b)
    return out


def reverse_bits(index, bits):
    out = 0
    for b in range(bits):
        out = out + ((index // (1 << b)) % 2) * (1 << (bits - 1 - b))
    return out


def z_roles():
    z = lax.axis_index("mpo")
    is_mid = (z == 1) | (z == 2)
    inner = jnp.where(z == 0, 1, 2)
    outer = jnp.where(z == 1, 0, 3)
    return z, is_mid, inner, outer, 3 - z


def site_kernel(bits, chunks, site, mixing, *refs):
    if mixing:
        (state, weight, ops, mask, out, gram,
         wbuf, psend, own, prec, xrec, cg, zsend, zrec,
         wsem, pss, prs, xss, xrs, zss, zrs) = refs
    else:
        (state, weight, gram, out, gram_out,
         wbuf, psend, own, prec, xrec, zown, zin, zsum, zrec,
         gsend, grec, gss, grs,
         wsem, pss, prs, xss, xrs, zss, zrs) = refs
    chips = 1 << bits
    depth = state.shape[1]
    rows = state.shape[0]
    block = weight.shape[2] // (2 * chips)
    width = block // chunks
    half = width // 2
    j = lax.axis_index("bond")
    me, core = j // 2, j % 2
    z, is_mid, inner, outer, across = z_roles()
    is_end = jnp.logical_not(is_mid)

    def weight_copy(c, other, r):
        dest = 2 * xor_bits(me, r, bits) + (1 - core if other else core)
        start = pl.multiple_of(dest * block + c * width, 128)
        slot = (c * 2 + (0 if other else 1)) * chips + r
        return pltpu.make_async_copy(
            weight.at[site, :, pl.ds(start, width)], wbuf.at[slot], wsem.at[slot]
        )

    for c in range(chunks):
        for other in (True, False):
            @pl.loop(0, chips)
            def _(r):
                weight_copy(c, other, r).start()

    barrier = pltpu.get_barrier_semaphore()

    def greet(bond, mpo):
        pl.semaphore_signal(barrier, inc=1, device_id=(bond, mpo), device_id_type=MESH)

    greet(2 * me + 1 - core, z)
    for b in range(bits):
        greet(2 * flip(me, b) + core, z)

    @pl.when(is_mid)
    def _():
        greet(j, outer)
        greet(j, across)
        pl.semaphore_wait(barrier, bits + 3)

    @pl.when(is_end)
    def _():
        greet(j, inner)
        pl.semaphore_wait(barrier, bits + 2)

    def remote(src, dst, ss, rs, bond, mpo):
        return pltpu.make_async_remote_copy(
            src_ref=src, dst_ref=dst, send_sem=ss, recv_sem=rs,
            device_id=(bond, mpo), device_id_type=MESH,
        )

    def pair_copy(c):
        return remote(psend.at[c], prec.at[c], pss.at[c], prs.at[c], 2 * me + 1 - core, z)

    def xy_copy(c, step, side):
        n = chips >> (step + 1)
        bit = bits - 1 - step if side == 0 else step
        return remote(
            own.at[c, side, pl.ds(n, n)], xrec.at[c, side, pl.ds(n, n)],
            xss.at[c, step, side], xrs.at[c, step, side], 2 * flip(me, bit) + core, z,
        )

    def multiply(c):
        for other, target in ((True, psend), (False, own)):
            @pl.loop(0, chips)
            def _(r):
                weight_copy(c, other, r).wait()
                slot = (c * 2 + (0 if other else 1)) * chips + r
                product = jnp.dot(state[...], wbuf[slot], preferred_element_type=F32).astype(BF16)
                target[c, 0, r] = product[:, :half]
                target[c, 1, reverse_bits(r, bits)] = product[:, half:]

            if other:
                pair_copy(c).start()

    def pair_sum(c):
        pair_copy(c).wait_recv()
        for side in range(2):
            own[c, side] = (own[c, side].astype(F32) + prec[c, side].astype(F32)).astype(BF16)
            xy_copy(c, 0, side).start()

    def xy_sum(c, step):
        n = chips >> (step + 1)
        parts = []
        for side in range(2):
            xy_copy(c, step, side).wait_recv()
            total = (own[c, side, pl.ds(0, n)].astype(F32)
                     + xrec[c, side, pl.ds(n, n)].astype(F32)).astype(BF16)
            if step < bits - 1:
                own[c, side, pl.ds(0, n)] = total
                xy_copy(c, step + 1, side).start()
            else:
                parts.append(total[0])
        return parts

    scale = 1.0 / weight.shape[2]
    columns = [pl.ds(c * width, width) for c in range(chunks)]

    if mixing:
        def z_end_copy(c, slot):
            return remote(cg.at[c, slot], cg.at[c, slot],
                          zss.at[c, 0], zrs.at[c, 0], j, jnp.where(is_mid, outer, inner))

        def z_own_copy(c, slot):
            return remote(cg.at[c, slot], cg.at[c, slot],
                          zss.at[c, 1], zrs.at[c, 1], j, jnp.where(is_mid, across, inner))

        def z_pass_copy(c, slot):
            return remote(cg.at[c, slot], cg.at[c, slot],
                          zss.at[c, 2], zrs.at[c, 2], j, jnp.where(is_mid, across, inner))

        def z_back_copy(c):
            return remote(zsend.at[c], zrec.at[c],
                          zss.at[c, 3], zrs.at[c, 3], j, jnp.where(is_mid, outer, inner))

        def z_first(c, parts):
            cg[c, z, :, pl.ds(0, half)] = parts[0]
            cg[c, z, :, pl.ds(half, half)] = parts[1]

            @pl.when(is_end)
            def _():
                z_end_copy(c, z).start()

            @pl.when(is_mid)
            def _():
                z_own_copy(c, z).start()

        def z_second(c):
            @pl.when(is_mid)
            def _():
                z_end_copy(c, outer).wait_recv()
                z_pass_copy(c, outer).start()

        def mix(c, which):
            total = jnp.dot(ops[site, which, 0], cg[c, 0], preferred_element_type=F32)
            for s in range(1, 4):
                total += jnp.dot(ops[site, which, s], cg[c, s], preferred_element_type=F32)
            return total

        def keep(c, mixed):
            kept = (mixed * mask[:, columns[c]]).astype(BF16)
            out[:, columns[c]] = kept
            square = lax.dot_general(kept, kept, (((1,), (1,)), ((), ())),
                                     preferred_element_type=F32)
            if c == 0:
                gram[...] = square
            else:
                gram[...] += square

        def z_third(c):
            @pl.when(is_mid)
            def _():
                z_own_copy(c, across).wait_recv()
                z_pass_copy(c, 3 - outer).wait_recv()
                zsend[c] = mix(c, 1).astype(BF16)
                z_back_copy(c).start()
                keep(c, mix(c, 0))

        def z_fourth(c):
            @pl.when(is_end)
            def _():
                z_back_copy(c).wait_recv()
                keep(c, zrec[c].astype(F32))

        end_sends = (lambda c: z_end_copy(c, z),)
        mid_sends = (lambda c: z_own_copy(c, z), lambda c: z_pass_copy(c, outer), z_back_copy)
    else:
        def z_end_copy(c):
            return remote(zown.at[c], zin.at[c],
                          zss.at[c, 0], zrs.at[c, 0], j, jnp.where(is_mid, outer, inner))

        def z_mid_copy(c):
            return remote(zsum.at[c], zrec.at[c],
                          zss.at[c, 1], zrs.at[c, 1], j, jnp.where(is_mid, across, inner))

        def z_back_copy(c):
            return remote(zown.at[c], zin.at[c],
                          zss.at[c, 2], zrs.at[c, 2], j, jnp.where(is_mid, outer, inner))

        def z_first(c, parts):
            zown[c, :, pl.ds(0, half)] = parts[0]
            zown[c, :, pl.ds(half, half)] = parts[1]

            @pl.when(is_end)
            def _():
                z_end_copy(c).start()

        def z_second(c):
            @pl.when(is_mid)
            def _():
                z_end_copy(c).wait_recv()
                zsum[c] = (zown[c].astype(F32) + zin[c].astype(F32)).astype(BF16)
                z_mid_copy(c).start()

        def z_third(c):
            @pl.when(is_mid)
            def _():
                z_mid_copy(c).wait_recv()
                total = (zsum[c].astype(F32) + zrec[c].astype(F32)).astype(BF16)
                zown[c] = total
                z_back_copy(c).start()
                out[:, columns[c]] = total

        def z_fourth(c):
            @pl.when(is_end)
            def _():
                z_back_copy(c).wait_recv()
                out[:, columns[c]] = zin[c]

        def gram_copy(i):
            bond, mpo = j, z
            if i == 0:
                bond = 2 * me + 1 - core
            elif i <= bits:
                bond = 2 * flip(me, i - 1) + core
            else:
                mpo = jnp.where(is_mid, across if i == bits + 2 else outer, inner)
            return remote(gsend.at[i], grec.at[i], gss.at[i], grs.at[i], bond, mpo)

        def gram_sum(i):
            return gsend[i].astype(F32) + grec[i].astype(F32)

        def gram_step(t):
            if t <= bits + 1:
                if t == 0:
                    gsend[t] = gram[...].astype(BF16)
                else:
                    gram_copy(t - 1).wait_recv()
                    gsend[t] = gram_sum(t - 1).astype(BF16)
                if t <= bits:
                    gram_copy(t).start()
                else:
                    @pl.when(is_end)
                    def _():
                        gram_copy(t).start()
            elif t <= bits + 3:
                @pl.when(is_mid)
                def _():
                    gram_copy(t - 1).wait_recv()
                    gsend[t] = gram_sum(t - 1).astype(BF16)
                    gram_copy(t).start()
                    if t == bits + 3:
                        gram_out[...] = gsend[t].astype(F32) * scale
            elif t == bits + 4:
                @pl.when(is_end)
                def _():
                    gram_copy(t - 1).wait_recv()
                    gram_out[...] = grec[t - 1].astype(F32) * scale

        end_sends, mid_sends = (z_end_copy,), (z_mid_copy, z_back_copy)

    stages = [multiply, pair_sum]
    for step in range(bits - 1):
        stages.append(functools.partial(xy_sum, step=step))
    stages += [lambda c: z_first(c, xy_sum(c, bits - 1)), z_second, z_third, z_fourth]
    for t in range(max(chunks + len(stages) - 1, bits + 5)):
        for number, stage in enumerate(stages):
            if 0 <= t - number < chunks:
                stage(t - number)
        if not mixing:
            gram_step(t)

    for c in range(chunks):
        pair_copy(c).wait_send()
        for step in range(bits):
            for side in range(2):
                xy_copy(c, step, side).wait_send()

        @pl.when(is_end)
        def _():
            for copy in end_sends:
                copy(c).wait_send()
            if not mixing and c == 0:
                gram_copy(bits + 1).wait_send()

        @pl.when(is_mid)
        def _():
            for copy in mid_sends:
                copy(c).wait_send()
            if not mixing and c == 0:
                for i in (bits + 2, bits + 3):
                    gram_copy(i).wait_send()

    if not mixing:
        for i in range(bits + 1):
            gram_copy(i).wait_send()


def apply_site(bits, site, mixing, state, weight, *extra):
    rows, depth = state.shape
    chips = 1 << bits
    block = weight.shape[2] // (2 * chips)
    chunks = max(1, block // 256)
    width = block // chunks
    half = width // 2
    vmem = pl.BlockSpec(memory_space=pltpu.VMEM)
    parts = pltpu.VMEM((chunks, 2, chips, rows, half), BF16)
    piece = pltpu.VMEM((chunks, rows, width), BF16)
    out_shape = [jax.ShapeDtypeStruct((rows, block), BF16)]
    out_shape.append(jax.ShapeDtypeStruct((rows, rows), F32))
    dma = pltpu.SemaphoreType.DMA
    if mixing:
        z_scratch = [pltpu.VMEM((chunks, 4, rows, width), BF16), piece, piece]
    else:
        gram_parts = pltpu.VMEM((bits + 4, rows, rows), BF16)
        z_scratch = [piece] * 4 + [gram_parts] * 2 + [dma((bits + 4,))] * 2
    z_copies = 4 if mixing else 3
    return pl.pallas_call(
        functools.partial(site_kernel, bits, chunks, site, mixing),
        out_shape=out_shape,
        in_specs=[vmem, pl.BlockSpec(memory_space=pl.ANY)] + [vmem] * len(extra),
        out_specs=[vmem] * len(out_shape),
        scratch_shapes=[
            pltpu.VMEM((2 * chips * chunks, depth, width), BF16),
            parts, parts, parts, parts,
            *z_scratch,
            dma((2 * chips * chunks,)),
            dma((chunks,)), dma((chunks,)),
            dma((chunks, bits, 2)), dma((chunks, bits, 2)),
            dma((chunks, z_copies)), dma((chunks, z_copies)),
        ],
        compiler_params=pltpu.CompilerParams(
            collective_id=2 * site + (0 if mixing else 1),
            has_side_effects=True,
            vmem_limit_bytes=48 * 1024 * 1024,
        ),
        cost_estimate=pl.CostEstimate(
            flops=2 * rows * depth * weight.shape[2],
            bytes_accessed=2 * depth * weight.shape[2],
            transcendentals=0,
        ),
    )(state, weight, *extra)


def operator_blocks(operator_tensors, rows):
    bonds = operator_tensors.shape[2]
    z, is_mid, inner, outer, across = z_roles()
    found = []
    for t in (z, jnp.where(is_mid, outer, inner)):
        found.append(lax.dynamic_slice_in_dim(operator_tensors, t * bonds, bonds, 3))
    ops = jnp.stack(found, axis=1).swapaxes(3, 4)
    keep = ((0, 0),) * 3
    blocks = []
    for l in range(LEFT_ROWS):
        place = (l * bonds, rows - (l + 1) * bonds)
        blocks.append(jnp.pad(ops, keep + (place, place)))
    return functools.reduce(jnp.add, blocks)


def chosen_columns(kept_columns, physical, block):
    index = kept_columns // physical - lax.axis_index("bond") * block
    mine = (kept_columns % physical) == lax.axis_index("mpo")
    high = jnp.where(mine & (index >= 0), index // 128, -1)
    low = index % 128
    high = (high[:, :, None] == jnp.arange(block // 128)).astype(BF16)
    low = (low[:, :, None] == jnp.arange(128)).astype(BF16)
    marks = jnp.einsum("khi,khj->kij", high, low, preferred_element_type=F32)
    return marks.reshape(kept_columns.shape[0], 1, block)


def solution(mesh):
    bits = (mesh.shape["bond"] // 2).bit_length() - 1

    def on_device(carried, site_tensors, operator_tensors, rotation, kept_columns):
        row_count, block = carried.shape
        rows = -(-row_count // 16) * 16
        physical = operator_tensors.shape[1]
        sites = site_tensors.reshape(site_tensors.shape[0], block, -1)
        turns = rotation.reshape(rotation.shape[0], block, -1)
        ops = operator_blocks(operator_tensors, rows)
        mask = chosen_columns(kept_columns, physical, block)
        state = jnp.pad(carried, ((0, rows - row_count), (0, 0)))
        grams = []
        for site in range(SITE_COUNT):
            kept, gram = apply_site(bits, site, True, state, sites, ops, mask[site])
            state, gram = apply_site(bits, site, False, kept, turns, gram)
            grams.append(gram[:row_count, :row_count])
        return state[:row_count], jnp.stack(grams)

    return jax.shard_map(
        on_device,
        mesh=mesh,
        in_specs=(
            P(None, "bond"),
            P(None, "bond", "mpo", None),
            P(),
            P(None, "bond", "mpo", None),
            P(),
        ),
        out_specs=(P(None, "bond"), P()),
        check_vma=False,
    )
```

```python
import functools

import jax
import jax.numpy as jnp
from jax import lax
from jax.experimental import pallas as pl
from jax.experimental.pallas import tpu as pltpu
from jax.sharding import PartitionSpec as P

LEFT_ROWS = 3
SITE_COUNT = 2
MESH = pl.DeviceIdType.MESH
F32 = jnp.float32
A_SCRATCH = 15
BF16 = jnp.bfloat16


def flip(index, bit):
    return index + (1 - 2 * ((index // (1 << bit)) % 2)) * (1 << bit)


def xor_bits(index, other, bits):
    out = 0
    for b in range(bits):
        out = out + (((index // (1 << b)) % 2 + (other // (1 << b)) % 2) % 2) * (1 << b)
    return out


def reverse_bits(index, bits):
    out = 0
    for b in range(bits):
        out = out + ((index // (1 << b)) % 2) * (1 << (bits - 1 - b))
    return out


def z_roles():
    z = lax.axis_index("mpo")
    is_mid = (z == 1) | (z == 2)
    inner = jnp.where(z == 0, 1, 2)
    outer = jnp.where(z == 1, 0, 3)
    return z, is_mid, inner, outer, 3 - z


def phase(bits, chunks, site, mixing, refs):
    if mixing:
        (state, weight, ops, mask, out, gram,
         wbuf, psend, own, prec, xrec, cg, zsend, zrec,
         wsem, pss, prs, xss, xrs, zss, zrs) = refs
    else:
        (state, weight, gram, out, gram_out,
         wbuf, psend, own, prec, xrec, zown, zin, zsum, zrec,
         gsend, grec, gss, grs,
         wsem, pss, prs, xss, xrs, zss, zrs) = refs
    chips = 1 << bits
    depth = state.shape[1]
    rows = state.shape[0]
    block = weight.shape[2] // (2 * chips)
    width = block // chunks
    half = width // 2
    j = lax.axis_index("bond")
    me, core = j // 2, j % 2
    z, is_mid, inner, outer, across = z_roles()
    is_end = jnp.logical_not(is_mid)

    def weight_copy(c, other, r):
        dest = 2 * xor_bits(me, r, bits) + (1 - core if other else core)
        start = pl.multiple_of(dest * block + c * width, 128)
        slot = (c * 2 + (0 if other else 1)) * chips + r
        return pltpu.make_async_copy(
            weight.at[site, :, pl.ds(start, width)], wbuf.at[slot], wsem.at[slot]
        )

    for c in range(chunks):
        for other in (True, False):
            @pl.loop(0, chips)
            def _(r):
                weight_copy(c, other, r).start()

    yield

    def remote(src, dst, ss, rs, bond, mpo):
        return pltpu.make_async_remote_copy(
            src_ref=src, dst_ref=dst, send_sem=ss, recv_sem=rs,
            device_id=(bond, mpo), device_id_type=MESH,
        )

    def pair_copy(c):
        return remote(psend.at[c], prec.at[c], pss.at[c], prs.at[c], 2 * me + 1 - core, z)

    def xy_copy(c, step, side):
        n = chips >> (step + 1)
        bit = bits - 1 - step if side == 0 else step
        return remote(
            own.at[c, side, pl.ds(n, n)], xrec.at[c, side, pl.ds(n, n)],
            xss.at[c, step, side], xrs.at[c, step, side], 2 * flip(me, bit) + core, z,
        )

    def multiply(c):
        for other, target in ((True, psend), (False, own)):
            @pl.loop(0, chips)
            def _(r):
                weight_copy(c, other, r).wait()
                slot = (c * 2 + (0 if other else 1)) * chips + r
                product = jnp.dot(state[...], wbuf[slot], preferred_element_type=F32).astype(BF16)
                target[c, 0, r] = product[:, :half]
                target[c, 1, reverse_bits(r, bits)] = product[:, half:]

            if other:
                pair_copy(c).start()

    def pair_sum(c):
        pair_copy(c).wait_recv()
        for side in range(2):
            own[c, side] = (own[c, side].astype(F32) + prec[c, side].astype(F32)).astype(BF16)
            xy_copy(c, 0, side).start()

    def xy_sum(c, step):
        n = chips >> (step + 1)
        parts = []
        for side in range(2):
            xy_copy(c, step, side).wait_recv()
            total = (own[c, side, pl.ds(0, n)].astype(F32)
                     + xrec[c, side, pl.ds(n, n)].astype(F32)).astype(BF16)
            if step < bits - 1:
                own[c, side, pl.ds(0, n)] = total
                xy_copy(c, step + 1, side).start()
            else:
                parts.append(total[0])
        return parts

    scale = 1.0 / weight.shape[2]
    columns = [pl.ds(c * width, width) for c in range(chunks)]

    if mixing:
        def z_end_copy(c, slot):
            return remote(cg.at[c, slot], cg.at[c, slot],
                          zss.at[c, 0], zrs.at[c, 0], j, jnp.where(is_mid, outer, inner))

        def z_own_copy(c, slot):
            return remote(cg.at[c, slot], cg.at[c, slot],
                          zss.at[c, 1], zrs.at[c, 1], j, jnp.where(is_mid, across, inner))

        def z_pass_copy(c, slot):
            return remote(cg.at[c, slot], cg.at[c, slot],
                          zss.at[c, 2], zrs.at[c, 2], j, jnp.where(is_mid, across, inner))

        def z_back_copy(c):
            return remote(zsend.at[c], zrec.at[c],
                          zss.at[c, 3], zrs.at[c, 3], j, jnp.where(is_mid, outer, inner))

        def z_first(c, parts):
            cg[c, z, :, pl.ds(0, half)] = parts[0]
            cg[c, z, :, pl.ds(half, half)] = parts[1]

            @pl.when(is_end)
            def _():
                z_end_copy(c, z).start()

            @pl.when(is_mid)
            def _():
                z_own_copy(c, z).start()

        def z_second(c):
            @pl.when(is_mid)
            def _():
                z_end_copy(c, outer).wait_recv()
                z_pass_copy(c, outer).start()

        def mix(c, which):
            total = jnp.dot(ops[site, which, 0], cg[c, 0], preferred_element_type=F32)
            for s in range(1, 4):
                total += jnp.dot(ops[site, which, s], cg[c, s], preferred_element_type=F32)
            return total

        def keep(c, mixed):
            kept = (mixed * mask[:, columns[c]]).astype(BF16)
            out[:, columns[c]] = kept
            square = lax.dot_general(kept, kept, (((1,), (1,)), ((), ())),
                                     preferred_element_type=F32)
            if c == 0:
                gram[...] = square
            else:
                gram[...] += square

        def z_third(c):
            @pl.when(is_mid)
            def _():
                z_own_copy(c, across).wait_recv()
                z_pass_copy(c, 3 - outer).wait_recv()
                zsend[c] = mix(c, 1).astype(BF16)
                z_back_copy(c).start()
                keep(c, mix(c, 0))

        def z_fourth(c):
            @pl.when(is_end)
            def _():
                z_back_copy(c).wait_recv()
                keep(c, zrec[c].astype(F32))

        end_sends = (lambda c: z_end_copy(c, z),)
        mid_sends = (lambda c: z_own_copy(c, z), lambda c: z_pass_copy(c, outer), z_back_copy)
    else:
        def z_end_copy(c):
            return remote(zown.at[c], zin.at[c],
                          zss.at[c, 0], zrs.at[c, 0], j, jnp.where(is_mid, outer, inner))

        def z_mid_copy(c):
            return remote(zsum.at[c], zrec.at[c],
                          zss.at[c, 1], zrs.at[c, 1], j, jnp.where(is_mid, across, inner))

        def z_back_copy(c):
            return remote(zown.at[c], zin.at[c],
                          zss.at[c, 2], zrs.at[c, 2], j, jnp.where(is_mid, outer, inner))

        def z_first(c, parts):
            zown[c, :, pl.ds(0, half)] = parts[0]
            zown[c, :, pl.ds(half, half)] = parts[1]

            @pl.when(is_end)
            def _():
                z_end_copy(c).start()

        def z_second(c):
            @pl.when(is_mid)
            def _():
                z_end_copy(c).wait_recv()
                zsum[c] = (zown[c].astype(F32) + zin[c].astype(F32)).astype(BF16)
                z_mid_copy(c).start()

        def z_third(c):
            @pl.when(is_mid)
            def _():
                z_mid_copy(c).wait_recv()
                total = (zsum[c].astype(F32) + zrec[c].astype(F32)).astype(BF16)
                zown[c] = total
                z_back_copy(c).start()
                out[:, columns[c]] = total

        def z_fourth(c):
            @pl.when(is_end)
            def _():
                z_back_copy(c).wait_recv()
                out[:, columns[c]] = zin[c]

        def gram_copy(i):
            bond, mpo = j, z
            if i == 0:
                bond = 2 * me + 1 - core
            elif i <= bits:
                bond = 2 * flip(me, i - 1) + core
            else:
                mpo = jnp.where(is_mid, across if i == bits + 2 else outer, inner)
            return remote(gsend.at[i], grec.at[i], gss.at[i], grs.at[i], bond, mpo)

        def gram_sum(i):
            return gsend[i].astype(F32) + grec[i].astype(F32)

        def gram_step(t):
            if t <= bits + 1:
                if t == 0:
                    gsend[t] = gram[...].astype(BF16)
                else:
                    gram_copy(t - 1).wait_recv()
                    gsend[t] = gram_sum(t - 1).astype(BF16)
                if t <= bits:
                    gram_copy(t).start()
                else:
                    @pl.when(is_end)
                    def _():
                        gram_copy(t).start()
            elif t <= bits + 3:
                @pl.when(is_mid)
                def _():
                    gram_copy(t - 1).wait_recv()
                    gsend[t] = gram_sum(t - 1).astype(BF16)
                    gram_copy(t).start()
                    if t == bits + 3:
                        gram_out[...] = gsend[t].astype(F32) * scale
            elif t == bits + 4:
                @pl.when(is_end)
                def _():
                    gram_copy(t - 1).wait_recv()
                    gram_out[...] = grec[t - 1].astype(F32) * scale

        end_sends, mid_sends = (z_end_copy,), (z_mid_copy, z_back_copy)

    stages = [multiply, pair_sum]
    for step in range(bits - 1):
        stages.append(functools.partial(xy_sum, step=step))
    stages += [lambda c: z_first(c, xy_sum(c, bits - 1)), z_second, z_third, z_fourth]
    for t in range(max(chunks + len(stages) - 1, bits + 5)):
        for number, stage in enumerate(stages):
            if 0 <= t - number < chunks:
                stage(t - number)
        if not mixing:
            gram_step(t)

    yield

    for c in range(chunks):
        pair_copy(c).wait_send()
        for step in range(bits):
            for side in range(2):
                xy_copy(c, step, side).wait_send()

        @pl.when(is_end)
        def _():
            for copy in end_sends:
                copy(c).wait_send()
            if not mixing and c == 0:
                gram_copy(bits + 1).wait_send()

        @pl.when(is_mid)
        def _():
            for copy in mid_sends:
                copy(c).wait_send()
            if not mixing and c == 0:
                for i in (bits + 2, bits + 3):
                    gram_copy(i).wait_send()

    if not mixing:
        for i in range(bits + 1):
            gram_copy(i).wait_send()


def greet_peers(bits):
    j = lax.axis_index("bond")
    me, core = j // 2, j % 2
    z, is_mid, inner, outer, across = z_roles()
    is_end = jnp.logical_not(is_mid)
    barrier = pltpu.get_barrier_semaphore()

    def greet(bond, mpo):
        pl.semaphore_signal(barrier, inc=1, device_id=(bond, mpo), device_id_type=MESH)

    greet(2 * me + 1 - core, z)
    for b in range(bits):
        greet(2 * flip(me, b) + core, z)

    @pl.when(is_mid)
    def _():
        greet(j, outer)
        greet(j, across)
        pl.semaphore_wait(barrier, bits + 3)

    @pl.when(is_end)
    def _():
        greet(j, inner)
        pl.semaphore_wait(barrier, bits + 2)


def site_kernel(bits, chunks, site, *refs):
    state, tensor, turn, ops, mask, out, gram_out, kept, gram = refs[:9]
    first, second = refs[9:9 + A_SCRATCH], refs[9 + A_SCRATCH:]
    phases = [
        phase(bits, chunks, site, True, (state, tensor, ops, mask, kept, gram, *first)),
        phase(bits, chunks, site, False, (kept, turn, gram, out, gram_out, *second)),
    ]
    for part in phases:
        next(part)
    greet_peers(bits)
    for part in phases:
        next(part)
    for part in phases:
        next(part, None)


def apply_site(bits, site, state, tensor, turn, ops, mask):
    rows, depth = state.shape
    chips = 1 << bits
    block = tensor.shape[2] // (2 * chips)
    chunks = max(1, block // 256)
    width = block // chunks
    dma = pltpu.SemaphoreType.DMA
    vmem = pl.BlockSpec(memory_space=pltpu.VMEM)
    hbm = pl.BlockSpec(memory_space=pl.ANY)
    parts = pltpu.VMEM((chunks, 2, chips, rows, width // 2), BF16)
    piece = pltpu.VMEM((chunks, rows, width), BF16)
    gram_parts = pltpu.VMEM((bits + 4, rows, rows), BF16)
    common = [pltpu.VMEM((2 * chips * chunks, depth, width), BF16)] + [parts] * 4

    def semaphores(z_copies):
        return [
            dma((2 * chips * chunks,)),
            dma((chunks,)), dma((chunks,)),
            dma((chunks, bits, 2)), dma((chunks, bits, 2)),
            dma((chunks, z_copies)), dma((chunks, z_copies)),
        ]

    first = common + [pltpu.VMEM((chunks, 4, rows, width), BF16), piece, piece] + semaphores(4)
    second = (common + [piece] * 4 + [gram_parts] * 2 + [dma((bits + 4,))] * 2
              + semaphores(3))
    return pl.pallas_call(
        functools.partial(site_kernel, bits, chunks, site),
        out_shape=[
            jax.ShapeDtypeStruct((rows, block), BF16),
            jax.ShapeDtypeStruct((rows, rows), F32),
        ],
        in_specs=[vmem, hbm, hbm, vmem, vmem],
        out_specs=[vmem] * 2,
        scratch_shapes=[
            pltpu.VMEM((rows, block), BF16), pltpu.VMEM((rows, rows), F32), *first, *second,
        ],
        compiler_params=pltpu.CompilerParams(
            collective_id=site,
            has_side_effects=True,
            vmem_limit_bytes=60 * 1024 * 1024,
        ),
        cost_estimate=pl.CostEstimate(
            flops=4 * rows * depth * tensor.shape[2],
            bytes_accessed=4 * depth * tensor.shape[2],
            transcendentals=0,
        ),
    )(state, tensor, turn, ops, mask)


def operator_blocks(operator_tensors, rows):
    bonds = operator_tensors.shape[2]
    z, is_mid, inner, outer, across = z_roles()
    found = []
    for t in (z, jnp.where(is_mid, outer, inner)):
        found.append(lax.dynamic_slice_in_dim(operator_tensors, t * bonds, bonds, 3))
    ops = jnp.stack(found, axis=1).swapaxes(3, 4)
    keep = ((0, 0),) * 3
    blocks = []
    for l in range(LEFT_ROWS):
        place = (l * bonds, rows - (l + 1) * bonds)
        blocks.append(jnp.pad(ops, keep + (place, place)))
    return functools.reduce(jnp.add, blocks)


def chosen_columns(kept_columns, physical, block):
    index = kept_columns // physical - lax.axis_index("bond") * block
    mine = (kept_columns % physical) == lax.axis_index("mpo")
    high = jnp.where(mine & (index >= 0), index // 128, -1)
    low = index % 128
    high = (high[:, :, None] == jnp.arange(block // 128)).astype(BF16)
    low = (low[:, :, None] == jnp.arange(128)).astype(BF16)
    marks = jnp.einsum("khi,khj->kij", high, low, preferred_element_type=F32)
    return marks.reshape(kept_columns.shape[0], 1, block)


def solution(mesh):
    bits = (mesh.shape["bond"] // 2).bit_length() - 1

    def on_device(carried, site_tensors, operator_tensors, rotation, kept_columns):
        row_count, block = carried.shape
        rows = -(-row_count // 16) * 16
        physical = operator_tensors.shape[1]
        sites = site_tensors.reshape(site_tensors.shape[0], block, -1)
        turns = rotation.reshape(rotation.shape[0], block, -1)
        ops = operator_blocks(operator_tensors, rows)
        mask = chosen_columns(kept_columns, physical, block)
        state = jnp.pad(carried, ((0, rows - row_count), (0, 0)))
        grams = []
        for site in range(SITE_COUNT):
            state, gram = apply_site(bits, site, state, sites, turns, ops, mask[site])
            grams.append(gram[:row_count, :row_count])
        return state[:row_count], jnp.stack(grams)

    return jax.shard_map(
        on_device,
        mesh=mesh,
        in_specs=(
            P(None, "bond"),
            P(None, "bond", "mpo", None),
            P(),
            P(None, "bond", "mpo", None),
            P(),
        ),
        out_specs=(P(None, "bond"), P()),
        check_vma=False,
    )
```
